32 devices in a mesh: sec: 4 (over x, core), dom: 8 (over z, y).
Axes of the slice: x: 2, y: 2, z: 4, core: 2. Of those that a mesh axis runs over, the one named last changes fastest.
Arguments:
- actuator_fields: float32 [16, 64, 4096], P(None, 'dom', 'sec'), may hold values from -6 to 6
- sensor_fields: float32 [8, 64, 4096], P(None, 'dom', 'sec'), may hold values from -6 to 6
- region_ids: int32 [64, 4096], P('dom', 'sec'), may hold values from 0 to 15
- stiffness_table: float32 [16], replicated, may hold values from 1 to 4
- density_table: float32 [16], replicated, may hold values from 1 to 2
- supported: int32 [10, 8, 32], P(None, 'dom', 'sec'), may hold values 0 or 1
Outputs:
- final_position: float32 [24, 64, 4096], P(None, 'dom', 'sec')
- cross: float32 [160, 80], P('sec')
The draws below stay inside these ranges and needn't reach their ends.
All inputs are finite; a program needn't handle non-finite values. No bound on the sum of `supported` on one device may be relied on, other than what follows from the above.
Results may differ from the reference program's by a relative error of at most 0.0028.
Values sent between devices are 32-bit elements; how exact they have to be, the bound alone decides.
A program may use at most 64 MiB of HBM per device.

```python
import math
import jax
import jax.numpy as jnp

CX = 8
TILE_Y = 128
STEPS = 20
ACT = 16
SENS = 8
REGIONS = 16
SNAPS = 10
NX = 64
NY = 4096
N_DOM = 8


def touch_ends(drawn, rng, least, largest):
    spot = [jax.random.randint(jax.random.fold_in(rng, axis), (), 0, length) for axis, length in enumerate(drawn.shape)]
    main_axis = drawn.shape.index(max(drawn.shape))
    neighbour = spot[:main_axis] + [(spot[main_axis] + 1) % drawn.shape[main_axis]] + spot[main_axis + 1:]
    return drawn.at[tuple(spot)].set(least).at[tuple(neighbour)].set(largest)


def block_scale(stream_key, dims, pieces, low, high):
    loudness, own = 1.0, jax.random.fold_in(stream_key, 6)
    for dim, parts in pieces:
        draws = jnp.exp(jax.random.uniform(jax.random.fold_in(own, dim), (parts,), jnp.float32, low / len(pieces), high / len(pieces)))
        loudness = loudness * jnp.repeat(draws, dims[dim] // parts).reshape([-1 if axis == dim else 1 for axis in range(len(dims))])
    return loudness


def scatter_about(stream_key, dims, deviation, limit, cuts=(), dtype=jnp.bfloat16):
    level = block_scale(stream_key, dims, cuts, -0.22, 0.18) if cuts else 1.0
    result = jax.random.normal(stream_key, dims, jnp.float32) * deviation * level
    return jnp.minimum(jnp.maximum(result, -limit), limit).astype(dtype)


def setup_inputs(seed: int = 0) -> dict:
    streams_of = jax.random.split(jax.random.key(seed), 7)
    return {
        "actuator_fields": scatter_about(streams_of[0], (ACT, NX, NY), 1.0, 6.0, ((1, 8), (2, 4)), jnp.float32),
        "sensor_fields": scatter_about(streams_of[1], (SENS, NX, NY), 1.0, 6.0, ((1, 8), (2, 4)), jnp.float32),
        "region_ids": touch_ends(jax.random.randint(streams_of[2], (NX, NY), 0, REGIONS), jax.random.fold_in(streams_of[2], 1), 0, REGIONS - 1).astype(jnp.int32),
        "stiffness_table": jnp.clip(jnp.exp(jax.random.uniform(streams_of[3], (REGIONS,), jnp.float32, math.log(1.0), math.log(4.0))), 1.0, 4.0),
        "density_table": jnp.clip(jnp.exp(jax.random.uniform(streams_of[4], (REGIONS,), jnp.float32, math.log(1.0), math.log(2.0))), 1.0, 2.0),
        "supported": touch_ends((jax.random.randint(streams_of[5], (SNAPS, N_DOM, NY // TILE_Y), 0, 3) < 2).astype(jnp.int32), jax.random.fold_in(streams_of[5], 1), 0, 1),
    }


def divergence(padded, stiff_pad):
    rows = padded.shape[-2] - 2
    cols = padded.shape[-1] - 2
    centre = padded[..., 1:1 + rows, 1:1 + cols]
    stiff_centre = stiff_pad[1:1 + rows, 1:1 + cols]
    total = jnp.zeros_like(centre)
    for first, second in ((0, 1), (2, 1), (1, 0), (1, 2)):
        nearby = padded[..., first:first + rows, second:second + cols]
        stiff_near = stiff_pad[first:first + rows, second:second + cols]
        total = total + 0.5 * (stiff_centre + stiff_near) * (nearby - centre)
    return total

def reference(actuator_fields, sensor_fields, region_ids, stiffness_table, density_table, supported):
    stiffness = stiffness_table[region_ids]
    inv_mass = 1.0 / density_table[region_ids]
    stiff_pad = jnp.pad(stiffness, 1)
    velocity = jnp.concatenate([actuator_fields, sensor_fields], 0) * inv_mass
    position = jnp.zeros_like(velocity)
    frames = []
    for step in range(STEPS):
        padded = jnp.pad(position, ((0, 0), (1, 1), (1, 1)))
        velocity = velocity + 0.35 * inv_mass * divergence(padded, stiff_pad)
        position = position + 0.35 * velocity
        if step % 2 == 1:
            mask_tiles = supported[step // 2]
            cells = jnp.repeat(jnp.repeat(mask_tiles, CX, axis=0), TILE_Y, axis=1).astype(jnp.float32)
            frames.append(jnp.stack([position * cells, velocity * cells], 1).astype(jnp.bfloat16))
    adjoint = jnp.stack([frame[ACT:].reshape(SENS, -1) for frame in frames], 1).reshape(SENS * SNAPS, -1)
    blocks = []
    for frame in frames:
        primal = frame[:ACT].reshape(ACT, -1)
        blocks.append(jnp.dot(primal, adjoint.T, preferred_element_type=jnp.float32))
    joined = jnp.stack(blocks, 1).reshape(ACT * SNAPS, SENS * SNAPS)
    cross = joined * (1.0 / math.sqrt(NX * NY))
    return (position, cross)
```

```python
import functools
import math

import jax
import jax.numpy as jnp
from jax import lax
from jax.experimental import pallas as pl
from jax.experimental.pallas import tpu as pltpu
from jax.sharding import PartitionSpec as P

TILE_Y = 128
ACT = 16
SNAPS = 10


def padded_2(cells, sides, width):
    for axis, dim in sides:
        count = lax.axis_size(axis)
        ends = count - 1
        head = lax.slice_in_dim(cells, 0, width, axis=dim)
        tail = lax.slice_in_dim(cells, cells.shape[dim] - width, cells.shape[dim], axis=dim)
        cells = jnp.concatenate(
            [
                lax.ppermute(tail, axis, [(i, (i + 1) % count) for i in range(ends)]),
                cells,
                lax.ppermute(head, axis, [((i + 1) % count, i) for i in range(ends)]),
            ],
            axis=dim,
        )
    return cells


def divergence(padded, stiff_pad):
    rows = padded.shape[-2] - 2
    cols = padded.shape[-1] - 2
    centre = padded[..., 1 : 1 + rows, 1 : 1 + cols]
    stiff_centre = stiff_pad[1 : 1 + rows, 1 : 1 + cols]
    total = jnp.zeros_like(centre)
    for first, second in ((0, 1), (2, 1), (1, 0), (1, 2)):
        nearby = padded[..., first : first + rows, second : second + cols]
        stiff_near = stiff_pad[first : first + rows, second : second + cols]
        total = total + 0.5 * (stiff_centre + stiff_near) * (nearby - centre)
    return total


def lookup(region_ids, table):
    labels = jnp.arange(table.shape[0], dtype=jnp.int32)
    match = (region_ids[None, :, :] == labels[:, None, None]).astype(jnp.float32)
    return jnp.sum(match * table[:, None, None], axis=0)


def body(actuator_fields, sensor_fields, region_ids, stiffness_table, density_table, supported):
    stiffness = lookup(region_ids, stiffness_table)
    inv_mass = 1.0 / lookup(region_ids, density_table)
    depth = 2
    stiff_pad, mass_pad = (
        padded_2(stiffness, (("sec", 1), ("dom", 0)), depth),
        padded_2(inv_mass, (("sec", 1), ("dom", 0)), depth),
    )
    velocity = jnp.concatenate([actuator_fields, sensor_fields], 0) * inv_mass
    position = jnp.zeros_like(velocity)
    count = velocity.shape[0]
    rows, cols = stiffness.shape
    frames = jnp.zeros((count, SNAPS, 2, rows, cols), jnp.bfloat16)

    def advance(position, velocity):
        pos_pad, vel_pad = (
            padded_2(position, (("sec", 2), ("dom", 1)), 2),
            padded_2(velocity, (("sec", 2), ("dom", 1)), 2),
        )
        vel_ext = vel_pad[:, 1:-1, 1:-1] + 0.35 * mass_pad[1:-1, 1:-1] * divergence(
            pos_pad, stiff_pad
        )
        pos_ext = pos_pad[:, 1:-1, 1:-1] + 0.35 * vel_ext
        velocity = vel_ext[:, 1:-1, 1:-1] + 0.35 * inv_mass * divergence(
            pos_ext, stiff_pad[1:-1, 1:-1]
        )
        return (pos_ext[:, 1:-1, 1:-1] + 0.35 * velocity, velocity)

    def pair_step(index, carry):
        position, velocity, frames = carry
        position, velocity = advance(position, velocity)
        mask_row = lax.dynamic_index_in_dim(supported, index, 0, keepdims=False)
        cells = jnp.repeat(mask_row, TILE_Y, axis=1).astype(jnp.float32)
        frame = jnp.stack([position * cells, velocity * cells], 1).astype(jnp.bfloat16)
        frames = lax.dynamic_update_slice_in_dim(frames, frame[:, None], index, 1)
        return (position, velocity, frames)

    position, velocity, frames = lax.fori_loop(0, SNAPS, pair_step, (position, velocity, frames))
    flat_frames = frames.reshape(count * SNAPS, 2 * rows * cols)
    primal = flat_frames[: ACT * SNAPS]
    adjoint = flat_frames[ACT * SNAPS :]
    local = lax.dot_general(
        primal, adjoint, (((1,), (1,)), ((), ())), preferred_element_type=jnp.float32
    )
    factor = 1.0 / math.sqrt(rows * cols * lax.axis_size("sec") * lax.axis_size("dom"))
    total = lax.psum(local, ("sec", "dom"))
    share = local.shape[0] // lax.axis_size("sec")
    block = lax.dynamic_slice_in_dim(total, lax.axis_index("sec") * share, share, 0)
    return (position, block * factor)


HALO = 24
LANES = 128
SUB = 8
MESH = pl.DeviceIdType.MESH


def wave_kernel(dims, act_ref, sens_ref, aux_ref, out_ref, part_ref,
                recv, field, coef, masks, pos_a, pos_b, vel, frames, back,
                in_send, in_recv, halo_send, halo_recv, out_send, out_recv):
    n_sec, n_dom, n_act, n_sens, steps = dims
    sec = lax.axis_index("sec")
    dom = lax.axis_index("dom")
    place = sec * n_dom + dom
    total = n_sec * n_dom
    n_resp = n_act + n_sens
    pairs = n_resp // 2
    act_pairs = n_act // 2
    sens_pairs = n_sens // 2
    core = LANES
    ext = core + 2 * HALO
    left = lax.rem(place + total - 1, total)
    right = lax.rem(place + 1, total)
    left_id = (left // n_dom, lax.rem(left, n_dom))
    right_id = (right // n_dom, lax.rem(right, n_dom))

    barrier = pltpu.get_barrier_semaphore()
    for off in range(1, n_dom):
        pl.semaphore_signal(barrier, inc=1, device_id=(sec, lax.rem(dom + off, n_dom)), device_id_type=MESH)
    pl.semaphore_signal(barrier, inc=1, device_id=left_id, device_id_type=MESH)
    pl.semaphore_signal(barrier, inc=1, device_id=right_id, device_id_type=MESH)
    pl.semaphore_wait(barrier, n_dom + 1)

    my_rows = pl.ds(pl.multiple_of(dom * SUB, SUB), SUB)
    my_cols = pl.ds(pl.multiple_of(dom * LANES, LANES), LANES)
    groups = ((aux_ref, n_resp, 3), (act_ref, 0, n_act), (sens_ref, n_act, n_sens))
    copies = []
    for g, (src, first, count) in enumerate(groups):
        for off in range(1, n_dom):
            peer = lax.rem(dom + off, n_dom)
            cols = pl.ds(pl.multiple_of(peer * LANES, LANES), LANES)
            copy = pltpu.make_async_remote_copy(
                src_ref=src.at[:, :, cols],
                dst_ref=recv.at[pl.ds(first, count), my_rows, :],
                send_sem=in_send.at[g, off - 1],
                recv_sem=in_recv.at[g, off - 1],
                device_id=(sec, peer),
                device_id_type=MESH,
            )
            copy.start()
            copies.append(copy)
    for src, first, count in groups:
        recv[pl.ds(first, count), my_rows, :] = src[:, :, my_cols]
    for copy in copies:
        copy.wait()

    inner = pl.ds(HALO, core)

    def flip(first, second):
        return jnp.concatenate([recv[first], recv[second]], 0).T

    for p in range(pairs):
        if p < act_pairs:
            first, second = p, p + act_pairs
        else:
            first = n_act + p - act_pairs
            second = first + sens_pairs
        field[p, inner, :] = flip(first, second)
    field[pairs, inner, :] = flip(n_resp, n_resp)
    field[pairs + 1, inner, :] = flip(n_resp + 1, n_resp + 1)
    masks[...] = flip(n_resp + 2, n_resp + 2)[: masks.shape[0], :]

    to_left = pltpu.make_async_remote_copy(
        src_ref=field.at[:, pl.ds(HALO, HALO), :],
        dst_ref=field.at[:, pl.ds(HALO + core, HALO), :],
        send_sem=halo_send.at[0], recv_sem=halo_recv.at[0],
        device_id=left_id, device_id_type=MESH,
    )
    to_right = pltpu.make_async_remote_copy(
        src_ref=field.at[:, pl.ds(core, HALO), :],
        dst_ref=field.at[:, pl.ds(0, HALO), :],
        send_sem=halo_send.at[1], recv_sem=halo_recv.at[1],
        device_id=right_id, device_id_type=MESH,
    )
    to_left.start()
    to_right.start()
    to_left.wait()
    to_right.wait()

    where = lax.broadcasted_iota(jnp.int32, (ext, LANES), 0)
    lane = lax.broadcasted_iota(jnp.int32, (ext, LANES), 1)
    height = LANES // 2
    row = lax.rem(lane, height)
    low = jnp.where(place == 0, HALO, 0)
    high = jnp.where(place == total - 1, HALO + core, ext)
    inside = (where >= low) & (where < high)
    stiff = jnp.where(inside, field[pairs], 0.0)
    mass = jnp.where(inside, field[pairs + 1], 0.0)
    scale = (0.35 * 0.35 * 0.5) * mass
    up_in = row > 0
    down_in = row < height - 1
    stiff_up = jnp.where(up_in, pltpu.roll(stiff, 1, 1), 0.0)
    stiff_down = jnp.where(down_in, pltpu.roll(stiff, LANES - 1, 1), 0.0)
    stiff_left = jnp.where(where > 0, pltpu.roll(stiff, 1, 0), 0.0)
    stiff_right = jnp.where(where < ext - 1, pltpu.roll(stiff, ext - 1, 0), 0.0)
    c_up = scale * (stiff + stiff_up)
    c_down = scale * (stiff + stiff_down)
    c_left = scale * (stiff + stiff_left)
    c_right = scale * (stiff + stiff_right)
    coef[0] = jnp.where(up_in, c_up, 0.0)
    coef[1] = jnp.where(down_in, c_down, 0.0)
    coef[2] = c_left
    coef[3] = c_right
    coef[4] = (c_up + c_down) + (c_left + c_right)
    coef[5] = 0.35 * mass

    n_tiles = ext // SUB
    group = pos_a.shape[0]
    snaps = steps // 2
    height_rows = pairs * snaps

    def advance(src, dst, store):
        for t in range(n_tiles):
            at = pl.ds(t * SUB, SUB)
            cs = [coef[c, at, :] for c in range(5)]
            for q in range(group):
                centre = src[q, pl.ds(SUB + t * SUB, SUB), :]
                before = src[q, pl.ds(SUB - 1 + t * SUB, SUB), :]
                after = src[q, pl.ds(SUB + 1 + t * SUB, SUB), :]
                gain = (cs[0] * pltpu.roll(centre, 1, 1) + cs[1] * pltpu.roll(centre, LANES - 1, 1)) + (
                    cs[2] * before + cs[3] * after
                )
                new_vel = vel[q, at, :] + (gain - cs[4] * centre)
                new_pos = centre + new_vel
                vel[q, at, :] = new_vel
                dst[q, pl.ds(SUB + t * SUB, SUB), :] = new_pos
                if store is not None:
                    store(q, t, new_pos, new_vel)

    pad = jnp.zeros((group, SUB, LANES), jnp.float32)
    for buf in (pos_a, pos_b):
        buf[:, pl.ds(0, SUB), :] = pad
        buf[:, pl.ds(SUB + ext, SUB), :] = pad

    def run_group(index, carry):
        for q in range(group):
            here = index * group + q
            vel[q] = jnp.where(inside, field[here] * coef[5], 0.0)
            pos_a[q, pl.ds(SUB, ext), :] = jnp.zeros((ext, LANES), jnp.float32)

        def pair_step(k, carry):
            mask = jnp.broadcast_to(masks[pl.ds(k, 1), :], (SUB, LANES))
            vmask = mask * (1.0 / 0.35)

            def store(q, t, new_pos, new_vel):
                if t * SUB < HALO or t * SUB >= HALO + core:
                    return
                y = t * SUB - HALO
                base = y * height_rows + (index * group + q) * snaps + k
                frames[pl.ds(base, SUB, stride=height_rows), :] = new_pos * mask
                frames[pl.ds(base + core * height_rows, SUB, stride=height_rows), :] = new_vel * vmask

            advance(pos_a, pos_b, None)
            advance(pos_b, pos_a, store)
            return carry

        lax.fori_loop(0, snaps, pair_step, 0)
        for q in range(group):
            back[index * group + q] = pos_a[q, pl.ds(SUB + HALO, core), :].T
        return carry

    lax.fori_loop(0, pairs // group, run_group, 0)

    sends = []
    parts = ((0, act_pairs, 0), (act_pairs, sens_pairs, n_act))
    for g, (first_pair, count, first) in enumerate(parts):
        for half in range(2):
            for off in range(1, n_dom):
                peer = lax.rem(dom + off, n_dom)
                rows = pl.ds(pl.multiple_of(half * height + peer * SUB, SUB), SUB)
                copy = pltpu.make_async_remote_copy(
                    src_ref=back.at[pl.ds(first_pair, count), rows, :],
                    dst_ref=out_ref.at[pl.ds(first + half * count, count), :, my_cols],
                    send_sem=out_send.at[2 * g + half, off - 1],
                    recv_sem=out_recv.at[2 * g + half, off - 1],
                    device_id=(sec, peer),
                    device_id_type=MESH,
                )
                copy.start()
                sends.append(copy)
            own = pl.ds(pl.multiple_of(half * height + dom * SUB, SUB), SUB)
            out_ref[pl.ds(first + half * count, count), :, my_cols] = back[pl.ds(first_pair, count), own, :]

    a_rows = act_pairs * snaps
    b_rows = sens_pairs * snaps
    half_a = lax.broadcasted_iota(jnp.int32, (a_rows, LANES), 1) < height

    def cross_step(index, acc):
        for part in range(2):
            lhs, rhs = [], []
            for side in range(2):
                base = pl.multiple_of((index * 4 + part * 2 + side) * height_rows, SUB)
                a = frames[pl.ds(base, a_rows), :]
                b = frames[pl.ds(base + a_rows, b_rows), :]
                lhs.append(jnp.concatenate([jnp.where(half_a, a, 0.0), jnp.where(half_a, 0.0, a)], 0).astype(jnp.bfloat16))
                rhs.append(jnp.concatenate([b, pltpu.roll(b, height, 1)], 0).astype(jnp.bfloat16))
            acc = acc + lax.dot_general(
                jnp.concatenate(lhs, 1), jnp.concatenate(rhs, 1), (((1,), (1,)), ((), ())),
                preferred_element_type=jnp.float32,
            )
        return acc

    acc = lax.fori_loop(0, 2 * core // 4, cross_step, jnp.zeros((2 * a_rows, 2 * b_rows), jnp.float32))
    factor = 1.0 / math.sqrt(height * core * total)
    acc = acc * factor
    part_ref[pl.ds(0, a_rows), :] = acc[:a_rows]
    part_ref[pl.ds(a_rows, a_rows), :] = jnp.concatenate([acc[a_rows:, b_rows:], acc[a_rows:, :b_rows]], 1)
    for copy in sends:
        copy.wait()


def fast_body(actuator_fields, sensor_fields, region_ids, stiffness_table, density_table, supported):
    stiffness = lookup(region_ids, stiffness_table)
    inv_mass = 1.0 / lookup(region_ids, density_table)
    snaps, _, tiles = supported.shape
    rows, cols = region_ids.shape
    mask = jnp.pad(supported[:, 0, :].T.astype(jnp.float32), ((0, 0), (0, LANES - snaps)))
    mask = jnp.broadcast_to(mask.reshape(1, tiles * LANES), (rows, cols))
    aux = jnp.stack([stiffness, inv_mass, mask], 0)
    n_sec, n_dom = lax.axis_size("sec"), lax.axis_size("dom")
    n_act, n_sens = actuator_fields.shape[0], sensor_fields.shape[0]
    n_resp = n_act + n_sens
    pairs = n_resp // 2
    ext = LANES + 2 * HALO
    group = 4
    f32 = jnp.float32
    vmem = pl.BlockSpec(memory_space=pltpu.VMEM)
    position, local = pl.pallas_call(
        functools.partial(wave_kernel, (n_sec, n_dom, n_act, n_sens, 2 * snaps)),
        out_shape=(
            jax.ShapeDtypeStruct((n_resp, rows, cols), f32),
            jax.ShapeDtypeStruct((n_act * snaps, n_sens * snaps), f32),
        ),
        in_specs=[vmem] * 3,
        out_specs=(vmem, vmem),
        scratch_shapes=[
            pltpu.VMEM((n_resp + 3, rows * n_dom, LANES), f32),
            pltpu.VMEM((pairs + 2, ext, LANES), f32),
            pltpu.VMEM((6, ext, LANES), f32),
            pltpu.VMEM((16, LANES), f32),
            pltpu.VMEM((group, ext + 2 * SUB, LANES), f32),
            pltpu.VMEM((group, ext + 2 * SUB, LANES), f32),
            pltpu.VMEM((group, ext, LANES), f32),
            pltpu.VMEM((2 * LANES * pairs * snaps, LANES), f32),
            pltpu.VMEM((pairs, LANES, LANES), f32),
            pltpu.SemaphoreType.DMA((3, n_dom - 1)),
            pltpu.SemaphoreType.DMA((3, n_dom - 1)),
            pltpu.SemaphoreType.DMA((2,)),
            pltpu.SemaphoreType.DMA((2,)),
            pltpu.SemaphoreType.DMA((4, n_dom - 1)),
            pltpu.SemaphoreType.DMA((4, n_dom - 1)),
        ],
        compiler_params=pltpu.CompilerParams(
            collective_id=0, has_side_effects=True, vmem_limit_bytes=48 * 1024 * 1024
        ),
    )(actuator_fields, sensor_fields, aux)
    total = lax.psum(local, ("sec", "dom"))
    share = local.shape[0] // n_sec
    return (position, lax.dynamic_slice_in_dim(total, lax.axis_index("sec") * share, share, 0))


def choose(*args):
    fields, _, region_ids, _, _, supported = args
    rows, cols = region_ids.shape
    n_dom = lax.axis_size("dom")
    fits = (
        rows == SUB
        and rows * n_dom * 2 == LANES
        and cols == LANES * n_dom
        and 2 * supported.shape[0] <= HALO
    )
    return fast_body(*args) if fits else body(*args)


def solution(mesh):
    in_specs = (
        P(None, "dom", "sec"),
        P(None, "dom", "sec"),
        P("dom", "sec"),
        P(),
        P(),
        P(None, "dom", "sec"),
    )
    out_specs = (P(None, "dom", "sec"), P("sec", None))
    return jax.shard_map(choose, mesh=mesh, in_specs=in_specs, out_specs=out_specs, check_vma=False)
```

```python
import functools
import math

import jax
import jax.numpy as jnp
from jax import lax
from jax.experimental import pallas as pl
from jax.experimental.pallas import tpu as pltpu
from jax.sharding import PartitionSpec as P

TILE_Y = 128
ACT = 16
SNAPS = 10


def padded_2(cells, sides, width):
    for axis, dim in sides:
        count = lax.axis_size(axis)
        ends = count - 1
        head = lax.slice_in_dim(cells, 0, width, axis=dim)
        tail = lax.slice_in_dim(cells, cells.shape[dim] - width, cells.shape[dim], axis=dim)
        cells = jnp.concatenate(
            [
                lax.ppermute(tail, axis, [(i, (i + 1) % count) for i in range(ends)]),
                cells,
                lax.ppermute(head, axis, [((i + 1) % count, i) for i in range(ends)]),
            ],
            axis=dim,
        )
    return cells


def divergence(padded, stiff_pad):
    rows = padded.shape[-2] - 2
    cols = padded.shape[-1] - 2
    centre = padded[..., 1 : 1 + rows, 1 : 1 + cols]
    stiff_centre = stiff_pad[1 : 1 + rows, 1 : 1 + cols]
    total = jnp.zeros_like(centre)
    for first, second in ((0, 1), (2, 1), (1, 0), (1, 2)):
        nearby = padded[..., first : first + rows, second : second + cols]
        stiff_near = stiff_pad[first : first + rows, second : second + cols]
        total = total + 0.5 * (stiff_centre + stiff_near) * (nearby - centre)
    return total


def lookup(region_ids, table):
    labels = jnp.arange(table.shape[0], dtype=jnp.int32)
    match = (region_ids[None, :, :] == labels[:, None, None]).astype(jnp.float32)
    return jnp.sum(match * table[:, None, None], axis=0)


def body(actuator_fields, sensor_fields, region_ids, stiffness_table, density_table, supported):
    stiffness = lookup(region_ids, stiffness_table)
    inv_mass = 1.0 / lookup(region_ids, density_table)
    depth = 2
    stiff_pad, mass_pad = (
        padded_2(stiffness, (("sec", 1), ("dom", 0)), depth),
        padded_2(inv_mass, (("sec", 1), ("dom", 0)), depth),
    )
    velocity = jnp.concatenate([actuator_fields, sensor_fields], 0) * inv_mass
    position = jnp.zeros_like(velocity)
    count = velocity.shape[0]
    rows, cols = stiffness.shape
    frames = jnp.zeros((count, SNAPS, 2, rows, cols), jnp.bfloat16)

    def advance(position, velocity):
        pos_pad, vel_pad = (
            padded_2(position, (("sec", 2), ("dom", 1)), 2),
            padded_2(velocity, (("sec", 2), ("dom", 1)), 2),
        )
        vel_ext = vel_pad[:, 1:-1, 1:-1] + 0.35 * mass_pad[1:-1, 1:-1] * divergence(
            pos_pad, stiff_pad
        )
        pos_ext = pos_pad[:, 1:-1, 1:-1] + 0.35 * vel_ext
        velocity = vel_ext[:, 1:-1, 1:-1] + 0.35 * inv_mass * divergence(
            pos_ext, stiff_pad[1:-1, 1:-1]
        )
        return (pos_ext[:, 1:-1, 1:-1] + 0.35 * velocity, velocity)

    def pair_step(index, carry):
        position, velocity, frames = carry
        position, velocity = advance(position, velocity)
        mask_row = lax.dynamic_index_in_dim(supported, index, 0, keepdims=False)
        cells = jnp.repeat(mask_row, TILE_Y, axis=1).astype(jnp.float32)
        frame = jnp.stack([position * cells, velocity * cells], 1).astype(jnp.bfloat16)
        frames = lax.dynamic_update_slice_in_dim(frames, frame[:, None], index, 1)
        return (position, velocity, frames)

    position, velocity, frames = lax.fori_loop(0, SNAPS, pair_step, (position, velocity, frames))
    flat_frames = frames.reshape(count * SNAPS, 2 * rows * cols)
    primal = flat_frames[: ACT * SNAPS]
    adjoint = flat_frames[ACT * SNAPS :]
    local = lax.dot_general(
        primal, adjoint, (((1,), (1,)), ((), ())), preferred_element_type=jnp.float32
    )
    factor = 1.0 / math.sqrt(rows * cols * lax.axis_size("sec") * lax.axis_size("dom"))
    total = lax.psum(local, ("sec", "dom"))
    share = local.shape[0] // lax.axis_size("sec")
    block = lax.dynamic_slice_in_dim(total, lax.axis_index("sec") * share, share, 0)
    return (position, block * factor)


HALO = 24
LANES = 128
SUB = 8
MESH = pl.DeviceIdType.MESH


def wave_kernel(dims, act_ref, sens_ref, aux_ref, out_ref, cross_ref,
                recv, field, coef, masks, pos_a, pos_b, vel, frames, back, part, by_sec, by_dom,
                in_send, in_recv, halo_send, halo_recv, out_send, out_recv,
                sec_send, sec_recv, dom_send, dom_recv):
    n_sec, n_dom, n_act, n_sens, steps = dims
    sec = lax.axis_index("sec")
    dom = lax.axis_index("dom")
    place = sec * n_dom + dom
    total = n_sec * n_dom
    n_resp = n_act + n_sens
    pairs = n_resp // 2
    group = pos_a.shape[0]
    members = 2 * group
    groups = n_resp // members
    core = LANES
    ext = core + 2 * HALO
    height = LANES // 2
    snaps = steps // 2
    height_rows = pairs * snaps
    left = lax.rem(place + total - 1, total)
    right = lax.rem(place + 1, total)
    left_id = (left // n_dom, lax.rem(left, n_dom))
    right_id = (right // n_dom, lax.rem(right, n_dom))

    barrier = pltpu.get_barrier_semaphore()
    for off in range(1, n_dom):
        pl.semaphore_signal(barrier, inc=1, device_id=(sec, lax.rem(dom + off, n_dom)), device_id_type=MESH)
    for off in range(1, n_sec):
        pl.semaphore_signal(barrier, inc=1, device_id=(lax.rem(sec + off, n_sec), dom), device_id_type=MESH)
    pl.semaphore_signal(barrier, inc=1, device_id=left_id, device_id_type=MESH)
    pl.semaphore_signal(barrier, inc=1, device_id=right_id, device_id_type=MESH)
    pl.semaphore_wait(barrier, n_dom + n_sec)

    my_rows = pl.ds(pl.multiple_of(dom * SUB, SUB), SUB)
    my_cols = pl.ds(pl.multiple_of(dom * LANES, LANES), LANES)

    def incoming(src, start, count, first, sem, off):
        peer = lax.rem(dom + off, n_dom)
        cols = pl.ds(pl.multiple_of(peer * LANES, LANES), LANES)
        return pltpu.make_async_remote_copy(
            src_ref=src.at[pl.ds(start, count), :, cols],
            dst_ref=recv.at[pl.ds(first, count), my_rows, :],
            send_sem=in_send.at[sem, off - 1],
            recv_sem=in_recv.at[sem, off - 1],
            device_id=(sec, peer),
            device_id_type=MESH,
        )

    sources = [(aux_ref, 0, 3, n_resp, groups)]
    for g in range(groups):
        at = g * members
        src, start = (act_ref, at) if at < n_act else (sens_ref, at - n_act)
        sources.append((src, start, members, at, g))
    arrivals = []
    for src, start, count, first, sem in sources:
        for off in range(1, n_dom):
            copy = incoming(src, start, count, first, sem, off)
            copy.start()
            arrivals.append(copy)
    for src, start, count, first, sem in sources:
        recv[pl.ds(first, count), my_rows, :] = src[pl.ds(start, count), :, my_cols]

    inner = pl.ds(HALO, core)

    def halo(count, first, sem):
        to_left = pltpu.make_async_remote_copy(
            src_ref=field.at[pl.ds(first, count), pl.ds(HALO, HALO), :],
            dst_ref=field.at[pl.ds(first, count), pl.ds(HALO + core, HALO), :],
            send_sem=halo_send.at[sem, 0], recv_sem=halo_recv.at[sem, 0],
            device_id=left_id, device_id_type=MESH,
        )
        to_right = pltpu.make_async_remote_copy(
            src_ref=field.at[pl.ds(first, count), pl.ds(core, HALO), :],
            dst_ref=field.at[pl.ds(first, count), pl.ds(0, HALO), :],
            send_sem=halo_send.at[sem, 1], recv_sem=halo_recv.at[sem, 1],
            device_id=right_id, device_id_type=MESH,
        )
        return to_left, to_right

    def group_halo(g):
        return halo(group, g * group, g)

    def aux_halo():
        return halo(2, pairs, groups)

    def flip(first, second):
        return jnp.concatenate([recv[first], recv[second]], 0).T

    def receive_group(g):
        for off in range(1, n_dom):
            incoming(act_ref, 0, members, g * members, g, off).wait_recv()
        for q in range(group):
            field[g * group + q, inner, :] = flip(g * members + q, g * members + group + q)
        for copy in group_halo(g):
            copy.start()

    for copy in arrivals[: n_dom - 1]:
        copy.wait_recv()
    field[pairs, inner, :] = flip(n_resp, n_resp)
    field[pairs + 1, inner, :] = flip(n_resp + 1, n_resp + 1)
    masks[...] = flip(n_resp + 2, n_resp + 2)[: masks.shape[0], :]
    for copy in aux_halo():
        copy.start()
    receive_group(0)
    for copy in aux_halo():
        copy.wait()

    where = lax.broadcasted_iota(jnp.int32, (ext, LANES), 0)
    lane = lax.broadcasted_iota(jnp.int32, (ext, LANES), 1)
    row = lax.rem(lane, height)
    low = jnp.where(place == 0, HALO, 0)
    high = jnp.where(place == total - 1, HALO + core, ext)
    inside = (where >= low) & (where < high)
    stiff = jnp.where(inside, field[pairs], 0.0)
    mass = jnp.where(inside, field[pairs + 1], 0.0)
    scale = (0.35 * 0.35 * 0.5) * mass
    up_in = row > 0
    down_in = row < height - 1
    stiff_up = jnp.where(up_in, pltpu.roll(stiff, 1, 1), 0.0)
    stiff_down = jnp.where(down_in, pltpu.roll(stiff, LANES - 1, 1), 0.0)
    stiff_left = jnp.where(where > 0, pltpu.roll(stiff, 1, 0), 0.0)
    stiff_right = jnp.where(where < ext - 1, pltpu.roll(stiff, ext - 1, 0), 0.0)
    c_up = scale * (stiff + stiff_up)
    c_down = scale * (stiff + stiff_down)
    c_left = scale * (stiff + stiff_left)
    c_right = scale * (stiff + stiff_right)
    coef[0] = jnp.where(up_in, c_up, 0.0)
    coef[1] = jnp.where(down_in, c_down, 0.0)
    coef[2] = c_left
    coef[3] = c_right
    coef[4] = (c_up + c_down) + (c_left + c_right)
    coef[5] = 0.35 * mass

    n_tiles = ext // SUB
    halo_tiles = HALO // SUB

    def advance(src, dst, skip, store):
        for t in range(skip, n_tiles - skip):
            at = pl.ds(t * SUB, SUB)
            cs = [coef[c, at, :] for c in range(5)]
            for q in range(group):
                centre = src[q, pl.ds(SUB + t * SUB, SUB), :]
                before = src[q, pl.ds(SUB - 1 + t * SUB, SUB), :]
                after = src[q, pl.ds(SUB + 1 + t * SUB, SUB), :]
                gain = (cs[0] * pltpu.roll(centre, 1, 1) + cs[1] * pltpu.roll(centre, LANES - 1, 1)) + (
                    cs[2] * before + cs[3] * after
                )
                new_vel = vel[q, at, :] + (gain - cs[4] * centre)
                new_pos = centre + new_vel
                vel[q, at, :] = new_vel
                dst[q, pl.ds(SUB + t * SUB, SUB), :] = new_pos
                if store is not None:
                    store(q, t, new_pos, new_vel)

    pad = jnp.zeros((group, SUB, LANES), jnp.float32)
    for buf in (pos_a, pos_b):
        buf[:, pl.ds(0, SUB), :] = pad
        buf[:, pl.ds(SUB + ext, SUB), :] = pad

    def outgoing(g, off):
        peer = lax.rem(dom + off, n_dom)
        rows = pl.ds(pl.multiple_of(peer * SUB, SUB), SUB)
        planes = pl.ds(g * members, members)
        return pltpu.make_async_remote_copy(
            src_ref=back.at[planes, rows, :],
            dst_ref=out_ref.at[planes, :, my_cols],
            send_sem=out_send.at[g, off - 1],
            recv_sem=out_recv.at[g, off - 1],
            device_id=(sec, peer),
            device_id_type=MESH,
        )

    def run_group(g, carry):
        for copy in group_halo(g):
            copy.wait()

        @pl.when(g < groups - 1)
        def _():
            receive_group(g + 1)

        for q in range(group):
            start = jnp.where(inside, field[g * group + q] * coef[5], 0.0)
            vel[q] = start
            pos_b[q, pl.ds(SUB, ext), :] = start

        def half_step(k, skip):
            mask = jnp.broadcast_to(masks[pl.ds(k, 1), :], (SUB, LANES))
            vmask = mask * (1.0 / 0.35)

            def store(q, t, new_pos, new_vel):
                if t < halo_tiles or t >= n_tiles - halo_tiles:
                    return
                y = (t - halo_tiles) * SUB
                base = y * height_rows + (g * group + q) * snaps + k
                frames[pl.ds(base, SUB, stride=height_rows), :] = new_pos * mask
                frames[pl.ds(base + core * height_rows, SUB, stride=height_rows), :] = new_vel * vmask

            advance(pos_b, pos_a, skip, store)

        half_step(0, 0)
        first = 1
        for skip in range(halo_tiles):
            last = first
            while last < snaps and (steps - 2 * last - 1 > (halo_tiles - 1 - skip) * SUB or skip == halo_tiles - 1):
                last += 1

            def pair_step(k, carry, skip=skip):
                advance(pos_a, pos_b, skip, None)
                half_step(k, skip)
                return carry

            if last > first:
                lax.fori_loop(first, last, pair_step, 0)
            first = last
        for q in range(group):
            turned = pos_a[q, pl.ds(SUB + HALO, core), :].T
            back[g * members + q] = turned[:height]
            back[g * members + group + q] = turned[height:]
        for off in range(1, n_dom):
            outgoing(g, off).start()
        return carry

    lax.fori_loop(0, groups, run_group, 0)
    out_ref[:, :, my_cols] = back[:, my_rows, :]

    a_pairs = n_act // 2
    a_rows = a_pairs * snaps
    b_rows = (pairs - a_pairs) * snaps
    half_a = lax.broadcasted_iota(jnp.int32, (a_rows, LANES), 1) < height

    def cross_step(index, acc):
        for piece in range(2):
            lhs, rhs = [], []
            for side in range(2):
                base = pl.multiple_of((index * 4 + piece * 2 + side) * height_rows, SUB)
                a = frames[pl.ds(base, a_rows), :]
                b = frames[pl.ds(base + a_rows, b_rows), :]
                lhs.append(jnp.concatenate([jnp.where(half_a, a, 0.0), jnp.where(half_a, 0.0, a)], 0).astype(jnp.bfloat16))
                rhs.append(jnp.concatenate([b, pltpu.roll(b, height, 1)], 0).astype(jnp.bfloat16))
            acc = acc + lax.dot_general(
                jnp.concatenate(lhs, 1), jnp.concatenate(rhs, 1), (((1,), (1,)), ((), ())),
                preferred_element_type=jnp.float32,
            )
        return acc

    acc = lax.fori_loop(0, 2 * core // 4, cross_step, jnp.zeros((2 * a_rows, 2 * b_rows), jnp.float32))
    second = jnp.concatenate([acc[a_rows:, b_rows:], acc[a_rows:, :b_rows]], 1)
    share = group * snaps
    for g in range(n_act // members):
        part[2 * g] = acc[g * share : (g + 1) * share]
        part[2 * g + 1] = second[g * share : (g + 1) * share]

    swaps = []
    for off in range(1, n_sec):
        peer = lax.rem(sec + off, n_sec)
        copy = pltpu.make_async_remote_copy(
            src_ref=part.at[peer], dst_ref=by_sec.at[sec],
            send_sem=sec_send.at[off - 1], recv_sem=sec_recv.at[off - 1],
            device_id=(peer, dom), device_id_type=MESH,
        )
        copy.start()
        swaps.append(copy)
    by_sec[sec] = part[sec]
    for copy in swaps:
        copy.wait()
    value = by_sec[0]
    for s in range(1, n_sec):
        value = value + by_sec[s]
    by_dom[dom] = value
    swaps = []
    for off in range(1, n_dom):
        copy = pltpu.make_async_remote_copy(
            src_ref=by_dom.at[dom], dst_ref=by_dom.at[dom],
            send_sem=dom_send.at[off - 1], recv_sem=dom_recv.at[off - 1],
            device_id=(sec, lax.rem(dom + off, n_dom)), device_id_type=MESH,
        )
        copy.start()
        swaps.append(copy)
    for copy in swaps:
        copy.wait()
    value = by_dom[0]
    for d in range(1, n_dom):
        value = value + by_dom[d]
    cross_ref[...] = value * (1.0 / math.sqrt(height * core * total))

    for copy in arrivals:
        copy.wait_send()
    for g in range(groups):
        for off in range(1, n_dom):
            outgoing(g, off).wait()


def fast_body(actuator_fields, sensor_fields, region_ids, stiffness_table, density_table, supported):
    stiffness = lookup(region_ids, stiffness_table)
    inv_mass = 1.0 / lookup(region_ids, density_table)
    snaps, _, tiles = supported.shape
    rows, cols = region_ids.shape
    mask = jnp.pad(supported[:, 0, :].T.astype(jnp.float32), ((0, 0), (0, LANES - snaps)))
    mask = jnp.broadcast_to(mask.reshape(1, tiles * LANES), (rows, cols))
    aux = jnp.stack([stiffness, inv_mass, mask], 0)
    n_sec, n_dom = lax.axis_size("sec"), lax.axis_size("dom")
    n_act, n_sens = actuator_fields.shape[0], sensor_fields.shape[0]
    n_resp = n_act + n_sens
    pairs = n_resp // 2
    ext = LANES + 2 * HALO
    group = 4
    f32 = jnp.float32
    vmem = pl.BlockSpec(memory_space=pltpu.VMEM)
    groups = pairs // group
    share = n_act * snaps // n_sec
    piece = (share, n_sens * snaps)
    sem = pltpu.SemaphoreType.DMA
    return pl.pallas_call(
        functools.partial(wave_kernel, (n_sec, n_dom, n_act, n_sens, 2 * snaps)),
        out_shape=(
            jax.ShapeDtypeStruct((n_resp, rows, cols), f32),
            jax.ShapeDtypeStruct(piece, f32),
        ),
        in_specs=[vmem] * 3,
        out_specs=(vmem, vmem),
        scratch_shapes=[
            pltpu.VMEM((n_resp + 3, rows * n_dom, LANES), f32),
            pltpu.VMEM((pairs + 2, ext, LANES), f32),
            pltpu.VMEM((6, ext, LANES), f32),
            pltpu.VMEM((16, LANES), f32),
            pltpu.VMEM((group, ext + 2 * SUB, LANES), f32),
            pltpu.VMEM((group, ext + 2 * SUB, LANES), f32),
            pltpu.VMEM((group, ext, LANES), f32),
            pltpu.VMEM((2 * LANES * pairs * snaps, LANES), f32),
            pltpu.VMEM((n_resp, rows * n_dom, LANES), f32),
            pltpu.VMEM((n_sec, *piece), f32),
            pltpu.VMEM((n_sec, *piece), f32),
            pltpu.VMEM((n_dom, *piece), f32),
            sem((groups + 1, n_dom - 1)),
            sem((groups + 1, n_dom - 1)),
            sem((groups + 1, 2)),
            sem((groups + 1, 2)),
            sem((groups, n_dom - 1)),
            sem((groups, n_dom - 1)),
            sem((n_sec - 1,)),
            sem((n_sec - 1,)),
            sem((n_dom - 1,)),
            sem((n_dom - 1,)),
        ],
        compiler_params=pltpu.CompilerParams(
            collective_id=0, has_side_effects=True, vmem_limit_bytes=48 * 1024 * 1024
        ),
    )(actuator_fields, sensor_fields, aux)


def choose(*args):
    fields, sensors, region_ids, _, _, supported = args
    rows, cols = region_ids.shape
    n_dom = lax.axis_size("dom")
    fits = (
        rows == SUB
        and rows * n_dom * 2 == LANES
        and cols == LANES * n_dom
        and 2 * supported.shape[0] <= HALO
        and fields.shape[0] == 4 * lax.axis_size("sec")
        and fields.shape[0] % 8 == 0
        and sensors.shape[0] == 8
    )
    return fast_body(*args) if fits else body(*args)


def solution(mesh):
    in_specs = (
        P(None, "dom", "sec"),
        P(None, "dom", "sec"),
        P("dom", "sec"),
        P(),
        P(),
        P(None, "dom", "sec"),
    )
    out_specs = (P(None, "dom", "sec"), P("sec", None))
    return jax.shard_map(choose, mesh=mesh, in_specs=in_specs, out_specs=out_specs, check_vma=False)
```

```python
import functools
import math

import jax
import jax.numpy as jnp
from jax import lax
from jax.experimental import pallas as pl
from jax.experimental.pallas import tpu as pltpu
from jax.sharding import PartitionSpec as P

TILE_Y = 128
ACT = 16
SNAPS = 10


def padded_2(cells, sides, width):
    for axis, dim in sides:
        count = lax.axis_size(axis)
        ends = count - 1
        head = lax.slice_in_dim(cells, 0, width, axis=dim)
        tail = lax.slice_in_dim(cells, cells.shape[dim] - width, cells.shape[dim], axis=dim)
        cells = jnp.concatenate(
            [
                lax.ppermute(tail, axis, [(i, (i + 1) % count) for i in range(ends)]),
                cells,
                lax.ppermute(head, axis, [((i + 1) % count, i) for i in range(ends)]),
            ],
            axis=dim,
        )
    return cells


def divergence(padded, stiff_pad):
    rows = padded.shape[-2] - 2
    cols = padded.shape[-1] - 2
    centre = padded[..., 1 : 1 + rows, 1 : 1 + cols]
    stiff_centre = stiff_pad[1 : 1 + rows, 1 : 1 + cols]
    total = jnp.zeros_like(centre)
    for first, second in ((0, 1), (2, 1), (1, 0), (1, 2)):
        nearby = padded[..., first : first + rows, second : second + cols]
        stiff_near = stiff_pad[first : first + rows, second : second + cols]
        total = total + 0.5 * (stiff_centre + stiff_near) * (nearby - centre)
    return total


def lookup(region_ids, table):
    labels = jnp.arange(table.shape[0], dtype=jnp.int32)
    match = (region_ids[None, :, :] == labels[:, None, None]).astype(jnp.float32)
    return jnp.sum(match * table[:, None, None], axis=0)


def body(actuator_fields, sensor_fields, region_ids, stiffness_table, density_table, supported):
    stiffness = lookup(region_ids, stiffness_table)
    inv_mass = 1.0 / lookup(region_ids, density_table)
    depth = 2
    stiff_pad, mass_pad = (
        padded_2(stiffness, (("sec", 1), ("dom", 0)), depth),
        padded_2(inv_mass, (("sec", 1), ("dom", 0)), depth),
    )
    velocity = jnp.concatenate([actuator_fields, sensor_fields], 0) * inv_mass
    position = jnp.zeros_like(velocity)
    count = velocity.shape[0]
    rows, cols = stiffness.shape
    frames = jnp.zeros((count, SNAPS, 2, rows, cols), jnp.bfloat16)

    def advance(position, velocity):
        pos_pad, vel_pad = (
            padded_2(position, (("sec", 2), ("dom", 1)), 2),
            padded_2(velocity, (("sec", 2), ("dom", 1)), 2),
        )
        vel_ext = vel_pad[:, 1:-1, 1:-1] + 0.35 * mass_pad[1:-1, 1:-1] * divergence(
            pos_pad, stiff_pad
        )
        pos_ext = pos_pad[:, 1:-1, 1:-1] + 0.35 * vel_ext
        velocity = vel_ext[:, 1:-1, 1:-1] + 0.35 * inv_mass * divergence(
            pos_ext, stiff_pad[1:-1, 1:-1]
        )
        return (pos_ext[:, 1:-1, 1:-1] + 0.35 * velocity, velocity)

    def pair_step(index, carry):
        position, velocity, frames = carry
        position, velocity = advance(position, velocity)
        mask_row = lax.dynamic_index_in_dim(supported, index, 0, keepdims=False)
        cells = jnp.repeat(mask_row, TILE_Y, axis=1).astype(jnp.float32)
        frame = jnp.stack([position * cells, velocity * cells], 1).astype(jnp.bfloat16)
        frames = lax.dynamic_update_slice_in_dim(frames, frame[:, None], index, 1)
        return (position, velocity, frames)

    position, velocity, frames = lax.fori_loop(0, SNAPS, pair_step, (position, velocity, frames))
    flat_frames = frames.reshape(count * SNAPS, 2 * rows * cols)
    primal = flat_frames[: ACT * SNAPS]
    adjoint = flat_frames[ACT * SNAPS :]
    local = lax.dot_general(
        primal, adjoint, (((1,), (1,)), ((), ())), preferred_element_type=jnp.float32
    )
    factor = 1.0 / math.sqrt(rows * cols * lax.axis_size("sec") * lax.axis_size("dom"))
    total = lax.psum(local, ("sec", "dom"))
    share = local.shape[0] // lax.axis_size("sec")
    block = lax.dynamic_slice_in_dim(total, lax.axis_index("sec") * share, share, 0)
    return (position, block * factor)


HALO = 24
LANES = 128
SUB = 8
MESH = pl.DeviceIdType.MESH


def wave_kernel(dims, act_ref, sens_ref, aux_ref, out_ref, cross_ref,
                recv, field, coef, masks, pos_a, pos_b, vel, frames, back, part, by_sec, by_dom,
                in_send, in_recv, halo_send, halo_recv, out_send, out_recv,
                sec_send, sec_recv, dom_send, dom_recv):
    n_sec, n_dom, n_act, n_sens, steps = dims
    sec = lax.axis_index("sec")
    dom = lax.axis_index("dom")
    place = sec * n_dom + dom
    total = n_sec * n_dom
    n_resp = n_act + n_sens
    pairs = n_resp // 2
    group = pos_a.shape[0]
    members = 2 * group
    groups = n_resp // members
    core = LANES
    ext = core + 2 * HALO
    height = LANES // 2
    snaps = steps // 2
    height_rows = pairs * snaps
    left = lax.rem(place + total - 1, total)
    right = lax.rem(place + 1, total)
    left_id = (left // n_dom, lax.rem(left, n_dom))
    right_id = (right // n_dom, lax.rem(right, n_dom))

    barrier = pltpu.get_barrier_semaphore()
    for off in range(1, n_dom):
        pl.semaphore_signal(barrier, inc=1, device_id=(sec, lax.rem(dom + off, n_dom)), device_id_type=MESH)
    for off in range(1, n_sec):
        pl.semaphore_signal(barrier, inc=1, device_id=(lax.rem(sec + off, n_sec), dom), device_id_type=MESH)
    pl.semaphore_signal(barrier, inc=1, device_id=left_id, device_id_type=MESH)
    pl.semaphore_signal(barrier, inc=1, device_id=right_id, device_id_type=MESH)
    pl.semaphore_wait(barrier, n_dom + n_sec)

    my_rows = pl.ds(pl.multiple_of(dom * SUB, SUB), SUB)
    my_cols = pl.ds(pl.multiple_of(dom * LANES, LANES), LANES)

    def incoming(src, start, count, first, sem, off):
        peer = lax.rem(dom + off, n_dom)
        cols = pl.ds(pl.multiple_of(peer * LANES, LANES), LANES)
        return pltpu.make_async_remote_copy(
            src_ref=src.at[pl.ds(start, count), :, cols],
            dst_ref=recv.at[pl.ds(first, count), my_rows, :],
            send_sem=in_send.at[sem, off - 1],
            recv_sem=in_recv.at[sem, off - 1],
            device_id=(sec, peer),
            device_id_type=MESH,
        )

    sources = [(aux_ref, 0, 3, n_resp, groups)]
    for g in range(groups):
        at = g * members
        src, start = (act_ref, at) if at < n_act else (sens_ref, at - n_act)
        sources.append((src, start, members, at, g))
    arrivals = []
    for src, start, count, first, sem in sources:
        for off in range(1, n_dom):
            copy = incoming(src, start, count, first, sem, off)
            copy.start()
            arrivals.append(copy)
    for src, start, count, first, sem in sources:
        recv[pl.ds(first, count), my_rows, :] = src[pl.ds(start, count), :, my_cols]

    inner = pl.ds(HALO, core)

    def halo(count, first, sem):
        to_left = pltpu.make_async_remote_copy(
            src_ref=field.at[pl.ds(first, count), pl.ds(HALO, HALO), :],
            dst_ref=field.at[pl.ds(first, count), pl.ds(HALO + core, HALO), :],
            send_sem=halo_send.at[sem, 0], recv_sem=halo_recv.at[sem, 0],
            device_id=left_id, device_id_type=MESH,
        )
        to_right = pltpu.make_async_remote_copy(
            src_ref=field.at[pl.ds(first, count), pl.ds(core, HALO), :],
            dst_ref=field.at[pl.ds(first, count), pl.ds(0, HALO), :],
            send_sem=halo_send.at[sem, 1], recv_sem=halo_recv.at[sem, 1],
            device_id=right_id, device_id_type=MESH,
        )
        return to_left, to_right

    def group_halo(g):
        return halo(group, g * group, g)

    def aux_halo():
        return halo(2, pairs, groups)

    def flip(first, second):
        return jnp.concatenate([recv[first], recv[second]], 0).T

    def receive_group(g):
        for off in range(1, n_dom):
            incoming(act_ref, 0, members, g * members, g, off).wait_recv()
        for q in range(group):
            field[g * group + q, inner, :] = flip(g * members + q, g * members + group + q)
        for copy in group_halo(g):
            copy.start()

    for copy in arrivals[: n_dom - 1]:
        copy.wait_recv()
    field[pairs, inner, :] = flip(n_resp, n_resp)
    field[pairs + 1, inner, :] = flip(n_resp + 1, n_resp + 1)
    masks[...] = flip(n_resp + 2, n_resp + 2)[: masks.shape[0], :]
    for copy in aux_halo():
        copy.start()
    receive_group(0)
    for copy in aux_halo():
        copy.wait()

    where = lax.broadcasted_iota(jnp.int32, (ext, LANES), 0)
    lane = lax.broadcasted_iota(jnp.int32, (ext, LANES), 1)
    row = lax.rem(lane, height)
    low = jnp.where(place == 0, HALO, 0)
    high = jnp.where(place == total - 1, HALO + core, ext)
    inside = (where >= low) & (where < high)
    stiff = jnp.where(inside, field[pairs], 0.0)
    mass = jnp.where(inside, field[pairs + 1], 0.0)
    scale = (0.35 * 0.35 * 0.5) * mass
    up_in = row > 0
    down_in = row < height - 1
    stiff_up = jnp.where(up_in, pltpu.roll(stiff, 1, 1), 0.0)
    stiff_down = jnp.where(down_in, pltpu.roll(stiff, LANES - 1, 1), 0.0)
    stiff_left = jnp.where(where > 0, pltpu.roll(stiff, 1, 0), 0.0)
    stiff_right = jnp.where(where < ext - 1, pltpu.roll(stiff, ext - 1, 0), 0.0)
    c_up = scale * (stiff + stiff_up)
    c_down = scale * (stiff + stiff_down)
    c_left = scale * (stiff + stiff_left)
    c_right = scale * (stiff + stiff_right)
    coef[0] = jnp.where(up_in, c_up, 0.0)
    coef[1] = jnp.where(down_in, c_down, 0.0)
    coef[2] = c_left
    coef[3] = c_right
    coef[4] = (c_up + c_down) + (c_left + c_right)
    coef[5] = 0.35 * mass

    n_tiles = ext // SUB
    halo_tiles = HALO // SUB

    def advance(src, dst, skip, store):
        for t in range(skip, n_tiles - skip):
            at = pl.ds(t * SUB, SUB)
            cs = [coef[c, at, :] for c in range(5)]
            for q in range(group):
                centre = src[q, pl.ds(SUB + t * SUB, SUB), :]
                before = src[q, pl.ds(SUB - 1 + t * SUB, SUB), :]
                after = src[q, pl.ds(SUB + 1 + t * SUB, SUB), :]
                gain = (cs[0] * pltpu.roll(centre, 1, 1) + cs[1] * pltpu.roll(centre, LANES - 1, 1)) + (
                    cs[2] * before + cs[3] * after
                )
                new_vel = vel[q, at, :] + (gain - cs[4] * centre)
                new_pos = centre + new_vel
                vel[q, at, :] = new_vel
                dst[q, pl.ds(SUB + t * SUB, SUB), :] = new_pos
                if store is not None:
                    store(q, t, new_pos, new_vel)

    pad = jnp.zeros((group, SUB, LANES), jnp.float32)
    for buf in (pos_a, pos_b):
        buf[:, pl.ds(0, SUB), :] = pad
        buf[:, pl.ds(SUB + ext, SUB), :] = pad

    def outgoing(g, off):
        peer = lax.rem(dom + off, n_dom)
        rows = pl.ds(pl.multiple_of(peer * SUB, SUB), SUB)
        planes = pl.ds(g * members, members)
        return pltpu.make_async_remote_copy(
            src_ref=back.at[planes, rows, :],
            dst_ref=out_ref.at[planes, :, my_cols],
            send_sem=out_send.at[g, off - 1],
            recv_sem=out_recv.at[g, off - 1],
            device_id=(sec, peer),
            device_id_type=MESH,
        )

    def run_group(g, carry):
        for copy in group_halo(g):
            copy.wait()

        for q in range(group):
            start = jnp.where(inside, field[g * group + q] * coef[5], 0.0)
            vel[q] = start
            pos_b[q, pl.ds(SUB, ext), :] = start

        def half_step(k, skip):
            mask = jnp.broadcast_to(masks[pl.ds(k, 1), :], (SUB, LANES))
            vmask = mask * (1.0 / 0.35)

            def store(q, t, new_pos, new_vel):
                if t < halo_tiles or t >= n_tiles - halo_tiles:
                    return
                y = (t - halo_tiles) * SUB
                base = y * height_rows + (g * group + q) * snaps + k
                frames[pl.ds(base, SUB, stride=height_rows), :] = new_pos * mask
                frames[pl.ds(base + core * height_rows, SUB, stride=height_rows), :] = new_vel * vmask

            advance(pos_b, pos_a, skip, store)

        half_step(0, 0)
        first = 1
        for skip in range(halo_tiles):
            last = first
            while last < snaps and (steps - 2 * last - 1 > (halo_tiles - 1 - skip) * SUB or skip == halo_tiles - 1):
                last += 1

            def pair_step(k, carry, skip=skip):
                advance(pos_a, pos_b, skip, None)
                half_step(k, skip)
                return carry

            if last > first:
                lax.fori_loop(first, last, pair_step, 0)
            first = last
            if skip == 1:

                @pl.when(g < groups - 1)
                def _():
                    receive_group(g + 1)

        for q in range(group):
            turned = pos_a[q, pl.ds(SUB + HALO, core), :].T
            back[g * members + q] = turned[:height]
            back[g * members + group + q] = turned[height:]
        for off in range(1, n_dom):
            outgoing(g, off).start()
        return carry

    lax.fori_loop(0, groups, run_group, 0)
    out_ref[:, :, my_cols] = back[:, my_rows, :]

    a_pairs = n_act // 2
    a_rows = a_pairs * snaps
    b_rows = (pairs - a_pairs) * snaps
    half_a = lax.broadcasted_iota(jnp.int32, (a_rows, LANES), 1) < height

    chunk = 32

    def cross_step(index, acc):
        lhs, rhs = [], []
        for side in range(chunk):
            base = pl.multiple_of((index * chunk + side) * height_rows, SUB)
            a = frames[pl.ds(base, a_rows), :]
            b = frames[pl.ds(base + a_rows, b_rows), :]
            lhs.append(jnp.concatenate([jnp.where(half_a, a, 0.0), jnp.where(half_a, 0.0, a)], 0).astype(jnp.bfloat16))
            rhs.append(jnp.concatenate([b, pltpu.roll(b, height, 1)], 0).astype(jnp.bfloat16))
        return acc + lax.dot_general(
            jnp.concatenate(lhs, 1), jnp.concatenate(rhs, 1), (((1,), (1,)), ((), ())),
            preferred_element_type=jnp.float32,
        )

    acc = lax.fori_loop(0, 2 * core // chunk, cross_step, jnp.zeros((2 * a_rows, 2 * b_rows), jnp.float32))
    second = jnp.concatenate([acc[a_rows:, b_rows:], acc[a_rows:, :b_rows]], 1)
    ordered = []
    for g in range(n_act // members):
        rows = slice(g * group * snaps, (g + 1) * group * snaps)
        ordered += [acc[rows], second[rows]]
    ordered = jnp.concatenate(ordered, 0)
    share = part.shape[1]
    for s in range(n_sec):
        part[s] = ordered[s * share : (s + 1) * share]

    swaps = []
    for off in range(1, n_sec):
        peer = lax.rem(sec + off, n_sec)
        copy = pltpu.make_async_remote_copy(
            src_ref=part.at[peer], dst_ref=by_sec.at[sec],
            send_sem=sec_send.at[off - 1], recv_sem=sec_recv.at[off - 1],
            device_id=(peer, dom), device_id_type=MESH,
        )
        copy.start()
        swaps.append(copy)
    by_sec[sec] = part[sec]
    for copy in swaps:
        copy.wait()
    value = by_sec[0]
    for s in range(1, n_sec):
        value = value + by_sec[s]
    by_dom[dom] = value
    swaps = []
    for off in range(1, n_dom):
        copy = pltpu.make_async_remote_copy(
            src_ref=by_dom.at[dom], dst_ref=by_dom.at[dom],
            send_sem=dom_send.at[off - 1], recv_sem=dom_recv.at[off - 1],
            device_id=(sec, lax.rem(dom + off, n_dom)), device_id_type=MESH,
        )
        copy.start()
        swaps.append(copy)
    for copy in swaps:
        copy.wait()
    value = by_dom[0]
    for d in range(1, n_dom):
        value = value + by_dom[d]
    value = value * (1.0 / math.sqrt(height * core * total))
    wide = group * snaps
    order = [
        value[:, h * b_rows + g * wide : h * b_rows + (g + 1) * wide] for g in range(n_sens // members) for h in range(2)
    ]
    cross_ref[...] = jnp.concatenate(order, 1)

    for copy in arrivals:
        copy.wait_send()
    for g in range(groups):
        for off in range(1, n_dom):
            outgoing(g, off).wait()


def fast_body(actuator_fields, sensor_fields, region_ids, stiffness_table, density_table, supported):
    stiffness = lookup(region_ids, stiffness_table)
    inv_mass = 1.0 / lookup(region_ids, density_table)
    snaps, _, tiles = supported.shape
    rows, cols = region_ids.shape
    mask = jnp.pad(supported[:, 0, :].T.astype(jnp.float32), ((0, 0), (0, LANES - snaps)))
    mask = jnp.broadcast_to(mask.reshape(1, tiles * LANES), (rows, cols))
    aux = jnp.stack([stiffness, inv_mass, mask], 0)
    n_sec, n_dom = lax.axis_size("sec"), lax.axis_size("dom")
    n_act, n_sens = actuator_fields.shape[0], sensor_fields.shape[0]
    n_resp = n_act + n_sens
    pairs = n_resp // 2
    ext = LANES + 2 * HALO
    group = 4
    f32 = jnp.float32
    vmem = pl.BlockSpec(memory_space=pltpu.VMEM)
    groups = pairs // group
    share = n_act * snaps // n_sec
    piece = (share, n_sens * snaps)
    sem = pltpu.SemaphoreType.DMA
    return pl.pallas_call(
        functools.partial(wave_kernel, (n_sec, n_dom, n_act, n_sens, 2 * snaps)),
        out_shape=(
            jax.ShapeDtypeStruct((n_resp, rows, cols), f32),
            jax.ShapeDtypeStruct(piece, f32),
        ),
        in_specs=[vmem] * 3,
        out_specs=(vmem, vmem),
        scratch_shapes=[
            pltpu.VMEM((n_resp + 3, rows * n_dom, LANES), f32),
            pltpu.VMEM((pairs + 2, ext, LANES), f32),
            pltpu.VMEM((6, ext, LANES), f32),
            pltpu.VMEM((16, LANES), f32),
            pltpu.VMEM((group, ext + 2 * SUB, LANES), f32),
            pltpu.VMEM((group, ext + 2 * SUB, LANES), f32),
            pltpu.VMEM((group, ext, LANES), f32),
            pltpu.VMEM((2 * LANES * pairs * snaps, LANES), f32),
            pltpu.VMEM((n_resp, rows * n_dom, LANES), f32),
            pltpu.VMEM((n_sec, *piece), f32),
            pltpu.VMEM((n_sec, *piece), f32),
            pltpu.VMEM((n_dom, *piece), f32),
            sem((groups + 1, n_dom - 1)),
            sem((groups + 1, n_dom - 1)),
            sem((groups + 1, 2)),
            sem((groups + 1, 2)),
            sem((groups, n_dom - 1)),
            sem((groups, n_dom - 1)),
            sem((n_sec - 1,)),
            sem((n_sec - 1,)),
            sem((n_dom - 1,)),
            sem((n_dom - 1,)),
        ],
        compiler_params=pltpu.CompilerParams(
            collective_id=0, has_side_effects=True, vmem_limit_bytes=48 * 1024 * 1024
        ),
    )(actuator_fields, sensor_fields, aux)


def choose(*args):
    fields, sensors, region_ids, _, _, supported = args
    rows, cols = region_ids.shape
    n_dom = lax.axis_size("dom")
    fits = (
        rows == SUB
        and rows * n_dom * 2 == LANES
        and cols == LANES * n_dom
        and 2 * supported.shape[0] <= HALO
        and fields.shape[0] == 4 * lax.axis_size("sec")
        and fields.shape[0] % 8 == 0
        and sensors.shape[0] == 8
    )
    return fast_body(*args) if fits else body(*args)


def solution(mesh):
    in_specs = (
        P(None, "dom", "sec"),
        P(None, "dom", "sec"),
        P("dom", "sec"),
        P(),
        P(),
        P(None, "dom", "sec"),
    )
    out_specs = (P(None, "dom", "sec"), P("sec", None))
    return jax.shard_map(choose, mesh=mesh, in_specs=in_specs, out_specs=out_specs, check_vma=False)
```
